128 devices in a mesh: prompt: 16 (over z, x_lo, core), resp: 8 (over y, x_hi).
Axes of the slice: x: 4 (x_hi: 2, x_lo: 2; x = x_hi * 2 + x_lo), y: 4, z: 4, core: 2. Of those that a mesh axis runs over, the one named last changes fastest.
Arguments:
- resp_q: bfloat16 [32, 512, 8192], P('prompt', None, 'resp'), may hold values from -40 to 40
- resp_k: bfloat16 [32, 512, 1024], P('prompt', None, 'resp'), may hold values from -13 to 13
- resp_v: bfloat16 [32, 512, 1024], P('prompt', None, 'resp'), may hold values from -6 to 6
- grad_out: bfloat16 [32, 512, 8192], P('prompt', None, 'resp'), may hold values from -6 to 6
- prefix_keys: bfloat16 [16384, 1024], P('prompt', 'resp'), may hold values from -6 to 6
- prefix_values: bfloat16 [16384, 1024], P('prompt', 'resp'), may hold values from -6 to 6
- slot_prompt: int32 [32], P('prompt'), may hold values from 0 to 15, as said below
- resp_len: int32 [32], P('prompt'), may hold values from 128 to 512, as said below
Outputs:
- query_grad: bfloat16 [32, 512, 8192], P('prompt', None, 'resp')
- resp_key_grad: bfloat16 [32, 512, 1024], P('prompt', None, 'resp')
- resp_value_grad: bfloat16 [32, 512, 1024], P('prompt', None, 'resp')
- prefix_key_grad: bfloat16 [16384, 1024], P('prompt', 'resp')
- prefix_value_grad: bfloat16 [16384, 1024], P('prompt', 'resp')
The draws below stay inside these ranges and needn't reach their ends.
Inputs may be any that keep to these rules, and one draw needn't show every extreme that they name: `slot_prompt`: every prompt is answered by at least one slot. `resp_len`: some slot's response fills all 512 rows.
All inputs are finite; a program needn't handle non-finite values.
Results may differ from the reference program's by a relative error of at most 0.013.
Values may be sent and summed in bfloat16 or wider, within the bound.
No kernel may reach another device: no remote copies, remote signals or barrier semaphores. Data moves between devices by JAX's collectives and lax.ppermute only.
A program may use at most 128 MiB of HBM per device.

```python
import math
import jax
import jax.numpy as jnp
from jax import lax

HQ = 64
HK = 8
DH = 128
L = 512
P_SIZE = 1024
S_DEV = 2
PROMPTS = 16
SLOTS = 32
PREFIX = 16384
N_PROMPT = 16


def draw_resp_k(key, part):
    key = jax.random.fold_in(key, 5)
    return jnp.clip(jax.random.normal(key, (SLOTS, L, HK * DH), jnp.float32), -4.0, 4.0).astype(jnp.bfloat16)


def draw_resp_q(key, part):
    key = jax.random.fold_in(key, 7)
    return jnp.clip(jax.random.normal(key, (SLOTS, L, HQ * DH), jnp.float32), -4.0, 4.0).astype(jnp.bfloat16)


def draw_slot_prompt(key, part):
    key = jax.random.fold_in(key, 11)
    first_keys = jax.random.split(key, 6)
    covering = jax.random.permutation(first_keys[0], PROMPTS).astype(jnp.int32)
    extra = SLOTS - PROMPTS
    choice_a = jax.random.randint(first_keys[1], (extra,), 0, PROMPTS)
    choice_b = jax.random.randint(first_keys[2], (extra,), 0, PROMPTS)
    choice_c = jax.random.randint(first_keys[3], (extra,), 0, PROMPTS)
    lowest = jnp.minimum(jnp.minimum(choice_a, choice_b), choice_c)
    relabel = jax.random.permutation(first_keys[4], PROMPTS).astype(jnp.int32)
    combined = jnp.concatenate([covering, relabel[lowest]]).astype(jnp.int32)
    shuffle = jax.random.permutation(first_keys[5], SLOTS)
    return combined[shuffle].astype(jnp.int32)


def draw_resp_len(key, part):
    key = jax.random.fold_in(key, 13)
    lengths = jax.random.randint(key, (SLOTS,), L // 4, L + 1).astype(jnp.int32)
    return lengths.at[0].set(L)


def steps_of(rng, shape, cuts, low, largest):
    gain = 1.0
    for position, shards_of in cuts:
        draws = jax.random.uniform(jax.random.fold_in(jax.random.fold_in(rng, 6), position), (shards_of,), jnp.float32, low / len(cuts), largest / len(cuts))
        gain = gain * jnp.repeat(jnp.exp(draws), shape[position] // shards_of).reshape((-1,) + (1,) * (len(shape) - 1 - position))
    return gain


def bell_draw(rng, shape, scale, bound, shards=(), held_as=jnp.bfloat16):
    values = scale * jax.random.normal(rng, shape, jnp.float32)
    if shards:
        values = values * steps_of(rng, shape, shards, -0.22, 0.18)
    return jnp.clip(values, -bound, bound).astype(held_as)


def setup_inputs(seed: int = 0) -> dict:
    keys = jax.random.split(jax.random.key(seed), 9)
    resp_q = draw_resp_q(jax.random.fold_in(keys[8], 71), 0)
    resp_k = draw_resp_k(jax.random.fold_in(keys[8], 71), 0)
    resp_v = bell_draw(keys[2], (SLOTS, L, HK * DH), 1.0, 6.0, ((0, 16), (2, 8)))
    grad_out = bell_draw(keys[3], (SLOTS, L, HQ * DH), 1.0, 6.0, ((0, 16), (2, 8)))
    prefix_keys = bell_draw(keys[4], (PREFIX, HK * DH), 1.0, 6.0, ((0, 16), (1, 8)))
    prefix_values = bell_draw(keys[5], (PREFIX, HK * DH), 1.0, 6.0, ((0, 16), (1, 8)))
    slot_prompt = draw_slot_prompt(jax.random.fold_in(keys[8], 71), 0)
    resp_len = draw_resp_len(jax.random.fold_in(keys[8], 71), 0)
    return dict(resp_q=resp_q, resp_k=resp_k, resp_v=resp_v, grad_out=grad_out, prefix_keys=prefix_keys, prefix_values=prefix_values, slot_prompt=slot_prompt, resp_len=resp_len)


def head_grad(query_rows, key_rows, value_rows, grad_rows, scaling):
    count_rows = query_rows.shape[0]
    count_keys = key_rows.shape[0]
    prefix_len = count_keys - count_rows
    scores = jnp.dot(query_rows, key_rows.T, preferred_element_type=jnp.float32) * scaling
    row_pos = jnp.arange(count_rows, dtype=jnp.int32)[:, None]
    col_pos = jnp.arange(count_keys, dtype=jnp.int32)[None, :]
    allowed = (col_pos < prefix_len) | (col_pos - prefix_len <= row_pos)
    scores = jnp.where(allowed, scores, jnp.float32(-1e+30))
    highest = lax.optimization_barrier(jnp.max(scores, axis=1, keepdims=True))
    expos = jnp.exp(scores - highest)
    attn_probs = expos / lax.optimization_barrier(jnp.sum(expos, axis=1, keepdims=True))
    rounded = attn_probs.astype(jnp.bfloat16)
    attended = jnp.dot(rounded, value_rows, preferred_element_type=jnp.float32)
    row_dot = lax.optimization_barrier(jnp.sum(grad_rows.astype(jnp.float32) * attended, axis=1, keepdims=True))
    grad_probs = jnp.dot(grad_rows, value_rows.T, preferred_element_type=jnp.float32)
    grad_scores = (attn_probs * (grad_probs - row_dot)).astype(jnp.bfloat16)
    query_grad = jnp.dot(grad_scores, key_rows, preferred_element_type=jnp.float32) * scaling
    key_grad = jnp.dot(grad_scores.T, query_rows, preferred_element_type=jnp.float32) * scaling
    value_grad = jnp.dot(rounded.T, grad_rows, preferred_element_type=jnp.float32)
    return (query_grad, key_grad, value_grad)

def slot_grads(query_rows, key_rows, value_rows, grad_rows):
    kv_heads = key_rows.shape[1] // DH
    q_heads = query_rows.shape[1] // DH
    group_size = q_heads // kv_heads
    scaling = 1.0 / math.sqrt(DH)
    initial = (jnp.zeros(query_rows.shape, jnp.float32), jnp.zeros(key_rows.shape, jnp.float32), jnp.zeros(key_rows.shape, jnp.float32))

    def one_head(head_index, carried):
        q_all, k_all, v_all = carried
        head_index = jnp.asarray(head_index, jnp.int32)
        offset_q = head_index * DH
        offset_kv = head_index // group_size * DH
        results = head_grad(lax.dynamic_slice_in_dim(query_rows, offset_q, DH, 1), lax.dynamic_slice_in_dim(key_rows, offset_kv, DH, 1), lax.dynamic_slice_in_dim(value_rows, offset_kv, DH, 1), lax.dynamic_slice_in_dim(grad_rows, offset_q, DH, 1), scaling)
        q_all = lax.dynamic_update_slice_in_dim(q_all, results[0], offset_q, 1)
        k_all = lax.dynamic_update_slice_in_dim(k_all, lax.dynamic_slice_in_dim(k_all, offset_kv, DH, 1) + results[1], offset_kv, 1)
        v_all = lax.dynamic_update_slice_in_dim(v_all, lax.dynamic_slice_in_dim(v_all, offset_kv, DH, 1) + results[2], offset_kv, 1)
        return (q_all, k_all, v_all)
    return lax.fori_loop(0, q_heads, one_head, initial)

def reference(resp_q, resp_k, resp_v, grad_out, prefix_keys, prefix_values, slot_prompt, resp_len):
    kv_width = HK * DH

    def one_slot(slot_items):
        queries, key_part, value_part, grad_rows, prompt_id, length = slot_items
        offset = (prompt_id * P_SIZE).astype(jnp.int32)
        key_rows = jnp.concatenate([lax.dynamic_slice_in_dim(prefix_keys, offset, P_SIZE, 0), key_part], 0)
        value_rows = jnp.concatenate([lax.dynamic_slice_in_dim(prefix_values, offset, P_SIZE, 0), value_part], 0)
        valid_rows = jnp.arange(L, dtype=jnp.int32) < length
        masked = jnp.where(valid_rows[:, None], grad_rows, jnp.zeros_like(grad_rows))
        q_all, k_all, v_all = slot_grads(queries, key_rows, value_rows, masked)
        return (q_all.astype(jnp.bfloat16), k_all[P_SIZE:].astype(jnp.bfloat16), v_all[P_SIZE:].astype(jnp.bfloat16), jnp.concatenate([k_all[:P_SIZE], v_all[:P_SIZE]], 1))
    query_grad, resp_key_grad, resp_value_grad, partials = lax.map(one_slot, (resp_q, resp_k, resp_v, grad_out, slot_prompt, resp_len))

    def add_group(group_id, totals):
        offset = (jnp.asarray(group_id, jnp.int32) * S_DEV).astype(jnp.int32)
        chosen = lax.dynamic_slice_in_dim(partials, offset, S_DEV, 0)
        owners = lax.dynamic_slice_in_dim(slot_prompt, offset, S_DEV, 0)
        onehot = (owners[:, None] == jnp.arange(PROMPTS, dtype=jnp.int32)[None, :]).astype(jnp.float32)
        partial_value = jnp.einsum('sp,sxf->pxf', onehot, chosen, precision=lax.Precision.HIGHEST)
        partial_value = lax.optimization_barrier(partial_value.astype(jnp.bfloat16))
        return totals + partial_value.astype(jnp.float32)
    totals = lax.fori_loop(0, N_PROMPT, add_group, jnp.zeros((PROMPTS, P_SIZE, 2 * kv_width), jnp.float32))
    totals = totals.reshape(PROMPTS * P_SIZE, 2 * kv_width)
    return (query_grad, resp_key_grad, resp_value_grad, totals[:, :kv_width].astype(jnp.bfloat16), totals[:, kv_width:].astype(jnp.bfloat16))
```

```python
import math

import jax
import jax.numpy as jnp
from jax import lax
from jax.experimental import pallas as pl
from jax.experimental.pallas import tpu as pltpu
from jax.sharding import PartitionSpec as P

DH = 128
L = 512
P_SIZE = 1024
KEYS = P_SIZE + L
ROWS = 256
TAG = 16
SCALE = 1.0 / math.sqrt(DH)
LOG2E = math.log2(math.e)
F32 = jnp.float32
BF16 = jnp.bfloat16


def dot(a, b, ca, cb):
    return lax.dot_general(a, b, (((ca,), (cb,)), ((), ())), preferred_element_type=F32)


def chunk_grads(q, g, k_all, v_all, t0, dk, dv):
    rows = q.shape[0]
    keys = P_SIZE + t0 + rows
    k = k_all[:keys]
    v = v_all[:keys]
    s = dot(q, k, 1, 1)
    ki = lax.broadcasted_iota(jnp.int32, (rows, rows), 1)
    ri = lax.broadcasted_iota(jnp.int32, (rows, rows), 0)
    tail = jnp.where(ki <= ri, s[:, P_SIZE + t0 :], -1e30)
    s = jnp.concatenate([s[:, : P_SIZE + t0], tail], 1)
    m = jnp.max(s, axis=1, keepdims=True)
    c = SCALE * LOG2E
    e = jnp.exp2(s * c - m * c)
    total = jnp.sum(e, axis=1, keepdims=True)
    gp = dot(g, v, 1, 1)
    p = e * (1.0 / total)
    row_dot = jnp.sum(p * gp, axis=1, keepdims=True)
    ds = (p * (gp - row_dot)).astype(BF16)
    dv[:, :keys] += dot(g, p.astype(BF16), 0, 0)
    dk[:, :keys] += dot(q, ds, 0, 0)
    return dot(ds, k, 1, 0)


def attn_body(len_ref, q_ref, g_ref, kp_ref, vp_ref, kr_ref, vr_ref, dq_ref, dkr_ref, dvr_ref, part_ref, kf, vf, dk, dv):
    slot = pl.program_id(0)
    head = pl.program_id(1)

    @pl.when(head == 0)
    def _():
        kf[:P_SIZE] = kp_ref[...].reshape(P_SIZE, DH)
        kf[P_SIZE:] = kr_ref[0]
        vf[:P_SIZE] = vp_ref[...].reshape(P_SIZE, DH)
        vf[P_SIZE:] = vr_ref[0]
        dk[...] = jnp.zeros_like(dk)
        dv[...] = jnp.zeros_like(dv)

    length = len_ref[slot]
    for t0 in range(0, L, ROWS):
        q = q_ref[0, t0 : t0 + ROWS]
        g = g_ref[0, t0 : t0 + ROWS]
        row = lax.broadcasted_iota(jnp.int32, (ROWS, DH), 0) + t0
        g = jnp.where(row < length, g, jnp.zeros_like(g))
        dq = chunk_grads(q, g, kf, vf, t0, dk, dv)
        dq_ref[0, t0 : t0 + ROWS] = (dq * SCALE).astype(BF16)

    @pl.when(head == pl.num_programs(1) - 1)
    def _():
        a = (dk[...] * SCALE).T.astype(BF16)
        b = dv[...].T.astype(BF16)
        dkr_ref[0] = a[P_SIZE:]
        dvr_ref[0] = b[P_SIZE:]
        pieces = part_ref.shape[0]
        part_ref[:, 0, :, :DH] = a[:P_SIZE].reshape(pieces, P_SIZE // pieces, DH)
        part_ref[:, 0, :, DH:] = b[:P_SIZE].reshape(pieces, P_SIZE // pieces, DH)


def attn(lens, q, g, kv, kr, vr):
    slots, heads = q.shape[0], q.shape[2] // DH
    n, _, piece, width = kv.shape
    column = lambda i, h, *_: (i, 0, h)
    slot = lambda i, h, *_: (i, 0, 0)
    return pl.pallas_call(
        attn_body,
        grid_spec=pltpu.PrefetchScalarGridSpec(
            num_scalar_prefetch=1,
            grid=(slots, heads),
            in_specs=[
                pl.BlockSpec((1, L, DH), column),
                pl.BlockSpec((1, L, DH), column),
                pl.BlockSpec((n, 1, piece, DH), lambda i, h, *_: (0, i, 0, 0)),
                pl.BlockSpec((n, 1, piece, DH), lambda i, h, *_: (0, i, 0, 1)),
                pl.BlockSpec((1, L, DH), slot),
                pl.BlockSpec((1, L, DH), slot),
            ],
            out_specs=[
                pl.BlockSpec((1, L, DH), column),
                pl.BlockSpec((1, L, DH), slot),
                pl.BlockSpec((1, L, DH), slot),
                pl.BlockSpec((n, 1, piece, width), lambda i, h, *_: (0, i, 0, 0)),
            ],
            scratch_shapes=[
                pltpu.VMEM((KEYS, DH), BF16),
                pltpu.VMEM((KEYS, DH), BF16),
                pltpu.VMEM((DH, KEYS), F32),
                pltpu.VMEM((DH, KEYS), F32),
            ],
        ),
        out_shape=[
            jax.ShapeDtypeStruct(q.shape, BF16),
            jax.ShapeDtypeStruct(kr.shape, BF16),
            jax.ShapeDtypeStruct(vr.shape, BF16),
            jax.ShapeDtypeStruct(kv.shape, BF16),
        ],
        compiler_params=pltpu.CompilerParams(
            dimension_semantics=("arbitrary", "arbitrary"), vmem_limit_bytes=40 << 20
        ),
        name="attn_grads",
    )(lens, q, g, kv, kv, kr, vr)


def pick_body(owner, pieces_ref, out_ref):
    n, slots, piece, _ = out_ref.shape
    for d in range(n):
        for i in range(slots):
            out_ref[d, i] = pieces_ref[owner[d * slots + i], :piece]


def pick(owner, pieces, slots):
    n, rows, width = pieces.shape
    return pl.pallas_call(
        pick_body,
        grid_spec=pltpu.PrefetchScalarGridSpec(
            num_scalar_prefetch=1,
            grid=(1,),
            in_specs=[pl.BlockSpec((n, rows, width), lambda i, *_: (0, 0, 0))],
            out_specs=pl.BlockSpec((n, slots, rows - TAG, width), lambda i, *_: (0, 0, 0, 0)),
        ),
        out_shape=jax.ShapeDtypeStruct((n, slots, rows - TAG, width), BF16),
        compiler_params=pltpu.CompilerParams(vmem_limit_bytes=16 << 20),
        name="pick_pieces",
    )(owner, pieces)


def total_body(owner, part_ref, out_ref, acc):
    n, slots, _, _ = part_ref.shape
    acc[...] = jnp.zeros_like(acc)
    for d in range(n):
        for i in range(slots):
            acc[owner[d * slots + i]] += part_ref[d, i].astype(F32)
    out_ref[...] = acc[...].astype(BF16)


def totals(owner, partials):
    n, slots, piece, width = partials.shape
    return pl.pallas_call(
        total_body,
        grid_spec=pltpu.PrefetchScalarGridSpec(
            num_scalar_prefetch=1,
            grid=(1,),
            in_specs=[pl.BlockSpec((n, slots, piece, width), lambda i, *_: (0, 0, 0, 0))],
            out_specs=pl.BlockSpec((n, piece, width), lambda i, *_: (0, 0, 0)),
            scratch_shapes=[pltpu.VMEM((n, piece, width), F32)],
        ),
        out_shape=jax.ShapeDtypeStruct((n, piece, width), BF16),
        compiler_params=pltpu.CompilerParams(vmem_limit_bytes=16 << 20),
        name="sum_partials",
    )(owner, partials)


def per_device(resp_q, resp_k, resp_v, grad_out, prefix_keys, prefix_values, slot_prompt, resp_len):
    slots = resp_q.shape[0]
    n = lax.axis_size("prompt")
    piece = P_SIZE // n

    def exchange(x):
        return lax.all_to_all(x, "prompt", 0, 0, tiled=True)

    kv = jnp.concatenate([prefix_keys, prefix_values], 1).reshape(n, piece, 2 * DH)
    tag = jnp.zeros((n, TAG, 2 * DH), BF16) + jnp.pad(slot_prompt.astype(BF16), (0, 2 * DH - slots))
    pieces = exchange(jnp.concatenate([kv, tag], 1))
    owner = pieces[:, piece, :slots].astype(jnp.int32).reshape(n * slots)
    kv = exchange(pick(owner, pieces, slots))
    query_grad, resp_key_grad, resp_value_grad, partials = attn(resp_len, resp_q, grad_out, kv, resp_k, resp_v)
    sums = exchange(totals(owner, exchange(partials)))
    return (
        query_grad,
        resp_key_grad,
        resp_value_grad,
        sums[:, :, :DH].reshape(P_SIZE, DH),
        sums[:, :, DH:].reshape(P_SIZE, DH),
    )


def solution(mesh):
    placed = (
        P("prompt", None, "resp"),
        P("prompt", None, "resp"),
        P("prompt", None, "resp"),
        P("prompt", None, "resp"),
        P("prompt", "resp"),
        P("prompt", "resp"),
        P("prompt"),
        P("prompt"),
    )
    return jax.shard_map(
        per_device,
        mesh=mesh,
        in_specs=placed,
        out_specs=(
            P("prompt", None, "resp"),
            P("prompt", None, "resp"),
            P("prompt", None, "resp"),
            P("prompt", "resp"),
            P("prompt", "resp"),
        ),
        check_vma=False,
    )
```

```python
import math

import jax
import jax.numpy as jnp
from jax import lax
from jax.experimental import pallas as pl
from jax.experimental.pallas import tpu as pltpu
from jax.sharding import PartitionSpec as P

DH = 128
L = 512
P_SIZE = 1024
KEYS = P_SIZE + L
ROWS = 128
HEADS_STEP = 8
ROWS_SOFTMAX = 32
VMEM_ATTN = 50 << 20
TAG = 8
SCALE = 1.0 / math.sqrt(DH)
LOG2E = math.log2(math.e)
F32 = jnp.float32
BF16 = jnp.bfloat16


def dot(a, b, ca, cb):
    return lax.dot_general(a, b, (((ca,), (cb,)), ((), ())), preferred_element_type=F32)


def attn_body(len_ref, q_ref, g_ref, kp_ref, vp_ref, kr_ref, vr_ref, dq_ref, dkr_ref, dvr_ref, part_ref, kf, vf, dk, dv, *buffers):
    slot = pl.program_id(0)
    group = pl.program_id(1)

    @pl.when(group == 0)
    def _():
        k_prefix = kp_ref[...].reshape(P_SIZE, DH)
        for side in range(2):
            kf[:P_SIZE, side * DH : (side + 1) * DH] = k_prefix
            kf[P_SIZE:, side * DH : (side + 1) * DH] = kr_ref[0]
        vf[:P_SIZE] = vp_ref[...].reshape(P_SIZE, DH)
        vf[P_SIZE:] = vr_ref[0]
        dk[...] = jnp.zeros_like(dk)
        dv[...] = jnp.zeros_like(dv)

    length = len_ref[slot]
    rows = HEADS_STEP * ROWS
    masked = lax.broadcasted_iota(jnp.int32, (ROWS, ROWS), 1) > lax.broadcasted_iota(jnp.int32, (ROWS, ROWS), 0)
    for c in range(L // ROWS):
        t0 = c * ROWS
        diag = P_SIZE + t0
        keys = diag + ROWS
        score, gprob, prob, dscore = [x.at[:, :keys] for x in buffers[4 * (c % 2) : 4 * (c % 2) + 4]]

        def stack(ref):
            return jnp.concatenate([ref[0, t0 : t0 + ROWS, h * DH : (h + 1) * DH] for h in range(HEADS_STEP)], 0)

        q = stack(q_ref)
        g = stack(g_ref)
        row = jnp.concatenate([lax.broadcasted_iota(jnp.int32, (ROWS, DH), 0) + t0] * HEADS_STEP, 0)
        g = jnp.where(row < length, g, jnp.zeros_like(g))
        scaled = q.astype(F32) * (SCALE * LOG2E)
        high = scaled.astype(BF16)
        low = (scaled - high.astype(F32)).astype(BF16)
        score[...] = dot(jnp.concatenate([high, low], 1), kf[:keys], 1, 1)
        gprob[...] = dot(g, vf[:keys], 1, 1)
        for h in range(HEADS_STEP):
            span = slice(h * ROWS, (h + 1) * ROWS)
            score[span, diag:] = jnp.where(masked, -1e30, score[span, diag:])
        inverse = []
        for r in range(0, rows, ROWS_SOFTMAX):
            span = slice(r, r + ROWS_SOFTMAX)
            s = score[span]
            gp = gprob[span]
            e = jnp.exp2(s - jnp.max(s, axis=1, keepdims=True))
            inv = 1.0 / jnp.sum(e, axis=1, keepdims=True)
            row_dot = jnp.sum(e * gp, axis=1, keepdims=True) * inv
            prob[span] = e.astype(BF16)
            dscore[span] = (e * (gp - row_dot)).astype(BF16)
            inverse.append(jnp.broadcast_to(inv, (ROWS_SOFTMAX, DH)))
        inv = jnp.concatenate(inverse, 0)
        dv[:, :keys] += dot((g.astype(F32) * inv).astype(BF16), prob[...], 0, 0)
        dk[:, :keys] += dot((q.astype(F32) * inv).astype(BF16), dscore[...], 0, 0)
        dq = (dot(dscore[...], kf[:keys, :DH], 1, 0) * (inv * SCALE)).astype(BF16)
        for h in range(HEADS_STEP):
            dq_ref[0, t0 : t0 + ROWS, h * DH : (h + 1) * DH] = dq[h * ROWS : (h + 1) * ROWS]

    @pl.when(group == pl.num_programs(1) - 1)
    def _():
        a = (dk[...] * SCALE).T.astype(BF16)
        b = dv[...].T.astype(BF16)
        dkr_ref[0] = a[P_SIZE:]
        dvr_ref[0] = b[P_SIZE:]
        pieces = part_ref.shape[0]
        part_ref[:, 0, :, :DH] = a[:P_SIZE].reshape(pieces, P_SIZE // pieces, DH)
        part_ref[:, 0, :, DH:] = b[:P_SIZE].reshape(pieces, P_SIZE // pieces, DH)


def attn(lens, q, g, kv, kr, vr):
    slots, heads = q.shape[0], q.shape[2] // DH
    n, _, piece, width = kv.shape
    rows = HEADS_STEP * ROWS
    column = lambda i, h, *_: (i, 0, h)
    slot = lambda i, h, *_: (i, 0, 0)
    return pl.pallas_call(
        attn_body,
        grid_spec=pltpu.PrefetchScalarGridSpec(
            num_scalar_prefetch=1,
            grid=(slots, heads // HEADS_STEP),
            in_specs=[
                pl.BlockSpec((1, L, HEADS_STEP * DH), column),
                pl.BlockSpec((1, L, HEADS_STEP * DH), column),
                pl.BlockSpec((n, 1, piece, DH), lambda i, h, *_: (0, i, 0, 0)),
                pl.BlockSpec((n, 1, piece, DH), lambda i, h, *_: (0, i, 0, 1)),
                pl.BlockSpec((1, L, DH), slot),
                pl.BlockSpec((1, L, DH), slot),
            ],
            out_specs=[
                pl.BlockSpec((1, L, HEADS_STEP * DH), column),
                pl.BlockSpec((1, L, DH), slot),
                pl.BlockSpec((1, L, DH), slot),
                pl.BlockSpec((n, 1, piece, width), lambda i, h, *_: (0, i, 0, 0)),
            ],
            scratch_shapes=[
                pltpu.VMEM((KEYS, 2 * DH), BF16),
                pltpu.VMEM((KEYS, DH), BF16),
                pltpu.VMEM((DH, KEYS), F32),
                pltpu.VMEM((DH, KEYS), F32),
            ]
            + [pltpu.VMEM((rows, KEYS), t) for t in (F32, F32, BF16, BF16)] * 2,
        ),
        out_shape=[
            jax.ShapeDtypeStruct(q.shape, BF16),
            jax.ShapeDtypeStruct(kr.shape, BF16),
            jax.ShapeDtypeStruct(vr.shape, BF16),
            jax.ShapeDtypeStruct(kv.shape, BF16),
        ],
        compiler_params=pltpu.CompilerParams(
            dimension_semantics=("arbitrary", "arbitrary"), vmem_limit_bytes=VMEM_ATTN
        ),
        name="attn_grads",
    )(lens, q, g, kv, kv, kr, vr)


def pick_body(owner, pieces_ref, out_ref):
    n, slots, piece, _ = out_ref.shape
    for d in range(n):
        for i in range(slots):
            out_ref[d, i] = pieces_ref[owner[d * slots + i], :piece]


def pick(owner, pieces, slots):
    n, rows, width = pieces.shape
    return pl.pallas_call(
        pick_body,
        grid_spec=pltpu.PrefetchScalarGridSpec(
            num_scalar_prefetch=1,
            grid=(1,),
            in_specs=[pl.BlockSpec((n, rows, width), lambda i, *_: (0, 0, 0))],
            out_specs=pl.BlockSpec((n, slots, rows - TAG, width), lambda i, *_: (0, 0, 0, 0)),
        ),
        out_shape=jax.ShapeDtypeStruct((n, slots, rows - TAG, width), BF16),
        compiler_params=pltpu.CompilerParams(vmem_limit_bytes=16 << 20),
        name="pick_pieces",
    )(owner, pieces)


def total_body(owner, part_ref, out_ref, acc):
    n, slots, _, _ = part_ref.shape
    acc[...] = jnp.zeros_like(acc)
    for d in range(n):
        for i in range(slots):
            acc[owner[d * slots + i]] += part_ref[d, i].astype(F32)
    out_ref[...] = acc[...].astype(BF16)


def totals(owner, partials):
    n, slots, piece, width = partials.shape
    return pl.pallas_call(
        total_body,
        grid_spec=pltpu.PrefetchScalarGridSpec(
            num_scalar_prefetch=1,
            grid=(1,),
            in_specs=[pl.BlockSpec((n, slots, piece, width), lambda i, *_: (0, 0, 0, 0))],
            out_specs=pl.BlockSpec((n, piece, width), lambda i, *_: (0, 0, 0)),
            scratch_shapes=[pltpu.VMEM((n, piece, width), F32)],
        ),
        out_shape=jax.ShapeDtypeStruct((n, piece, width), BF16),
        compiler_params=pltpu.CompilerParams(vmem_limit_bytes=16 << 20),
        name="sum_partials",
    )(owner, partials)


def per_device(resp_q, resp_k, resp_v, grad_out, prefix_keys, prefix_values, slot_prompt, resp_len):
    slots = resp_q.shape[0]
    n = lax.axis_size("prompt")
    piece = P_SIZE // n

    def exchange(x):
        return lax.all_to_all(x, "prompt", 0, 0, tiled=True)

    kv = jnp.concatenate([prefix_keys, prefix_values], 1).reshape(n, piece, 2 * DH)
    tag = jnp.zeros((n, TAG, 2 * DH), BF16) + jnp.pad(slot_prompt.astype(BF16), (0, 2 * DH - slots))
    pieces = exchange(jnp.concatenate([kv, tag], 1))
    owner = pieces[:, piece, :slots].astype(jnp.int32).reshape(n * slots)
    kv = exchange(pick(owner, pieces, slots))
    query_grad, resp_key_grad, resp_value_grad, partials = attn(resp_len, resp_q, grad_out, kv, resp_k, resp_v)
    sums = exchange(totals(owner, exchange(partials)))
    return (
        query_grad,
        resp_key_grad,
        resp_value_grad,
        sums[:, :, :DH].reshape(P_SIZE, DH),
        sums[:, :, DH:].reshape(P_SIZE, DH),
    )


def solution(mesh):
    placed = (
        P("prompt", None, "resp"),
        P("prompt", None, "resp"),
        P("prompt", None, "resp"),
        P("prompt", None, "resp"),
        P("prompt", "resp"),
        P("prompt", "resp"),
        P("prompt"),
        P("prompt"),
    )
    return jax.shard_map(
        per_device,
        mesh=mesh,
        in_specs=placed,
        out_specs=(
            P("prompt", None, "resp"),
            P("prompt", None, "resp"),
            P("prompt", None, "resp"),
            P("prompt", "resp"),
            P("prompt", "resp"),
        ),
        check_vma=False,
    )
```

```python
import functools
import math

import jax
import jax.numpy as jnp
from jax import lax
from jax.experimental import pallas as pl
from jax.experimental.pallas import tpu as pltpu
from jax.sharding import PartitionSpec as P

DH = 128
L = 512
P_SIZE = 1024
KEYS = P_SIZE + L
ROWS = 128
HEADS_STEP = 8
ROWS_SOFTMAX = 32
VMEM_ATTN = 46 << 20
TAG = 8
SCALE = 1.0 / math.sqrt(DH)
LOG2E = math.log2(math.e)
F32 = jnp.float32
BF16 = jnp.bfloat16


def dot(a, b, ca, cb):
    return lax.dot_general(a, b, (((ca,), (cb,)), ((), ())), preferred_element_type=F32)


def attn_body(width_q, len_ref, q_ref, g_ref, kp_ref, vp_ref, kr_ref, vr_ref, dq_ref, dkr_ref, dvr_ref, part_ref, kf, vf, dk, dv, *buffers):
    slot = pl.program_id(0)
    group = pl.program_id(1)

    @pl.when(group == 0)
    def _():
        k_prefix = kp_ref[...].reshape(P_SIZE, DH)
        for side in range(2):
            kf[:P_SIZE, side * DH : (side + 1) * DH] = k_prefix
            kf[P_SIZE:, side * DH : (side + 1) * DH] = kr_ref[0]
        vf[:P_SIZE] = vp_ref[...].reshape(P_SIZE, DH)
        vf[P_SIZE:] = vr_ref[0]
        if HEADS_STEP * DH != width_q:
            dk[...] = jnp.zeros_like(dk)
            dv[...] = jnp.zeros_like(dv)

    length = len_ref[slot]
    rows = HEADS_STEP * ROWS
    masked = lax.broadcasted_iota(jnp.int32, (ROWS, ROWS), 1) > lax.broadcasted_iota(jnp.int32, (ROWS, ROWS), 0)
    for c in reversed(range(L // ROWS)):
        t0 = c * ROWS
        diag = P_SIZE + t0
        keys = diag + ROWS
        score, gprob, prob, dscore = [x.at[:, :keys] for x in buffers[4 * (c % 2) : 4 * (c % 2) + 4]]

        def stack(ref):
            return jnp.concatenate([ref[0, t0 : t0 + ROWS, h * DH : (h + 1) * DH] for h in range(HEADS_STEP)], 0)

        q = stack(q_ref)
        g = stack(g_ref)
        row = jnp.concatenate([lax.broadcasted_iota(jnp.int32, (ROWS, DH), 0) + t0] * HEADS_STEP, 0)
        g = jnp.where(row < length, g, jnp.zeros_like(g))
        scaled = q.astype(F32) * (SCALE * LOG2E)
        high = scaled.astype(BF16)
        low = (scaled - high.astype(F32)).astype(BF16)
        score[...] = dot(jnp.concatenate([high, low], 1), kf[:keys], 1, 1)
        gprob[...] = dot(g, vf[:keys], 1, 1)
        for h in range(HEADS_STEP):
            span = slice(h * ROWS, (h + 1) * ROWS)
            score[span, diag:] = jnp.where(masked, -1e30, score[span, diag:])
        inverse = []
        for r in range(0, rows, ROWS_SOFTMAX):
            span = slice(r, r + ROWS_SOFTMAX)
            s = score[span]
            gp = gprob[span]
            e = jnp.exp2(s - jnp.max(s, axis=1, keepdims=True))
            inv = 1.0 / jnp.sum(e, axis=1, keepdims=True)
            row_dot = jnp.sum(e * gp, axis=1, keepdims=True) * inv
            prob[span] = e.astype(BF16)
            dscore[span] = (e * (gp - row_dot)).astype(BF16)
            inverse.append(jnp.broadcast_to(inv, (ROWS_SOFTMAX, DH)))
        inv = jnp.concatenate(inverse, 0)
        dv_part = dot((g.astype(F32) * inv).astype(BF16), prob[...], 0, 0)
        dk_part = dot((q.astype(F32) * inv).astype(BF16), dscore[...], 0, 0)
        if keys == KEYS and HEADS_STEP * DH == width_q:
            dv[...] = dv_part
            dk[...] = dk_part
        else:
            dv[:, :keys] += dv_part
            dk[:, :keys] += dk_part
        dq = (dot(dscore[...], kf[:keys, :DH], 1, 0) * (inv * SCALE)).astype(BF16)
        for h in range(HEADS_STEP):
            dq_ref[0, t0 : t0 + ROWS, h * DH : (h + 1) * DH] = dq[h * ROWS : (h + 1) * ROWS]

    @pl.when(group == pl.num_programs(1) - 1)
    def _():
        a = (dk[...] * SCALE).T.astype(BF16)
        b = dv[...].T.astype(BF16)
        dkr_ref[0] = a[P_SIZE:]
        dvr_ref[0] = b[P_SIZE:]
        pieces = part_ref.shape[0]
        part_ref[:, 0, :, :DH] = a[:P_SIZE].reshape(pieces, P_SIZE // pieces, DH)
        part_ref[:, 0, :, DH:] = b[:P_SIZE].reshape(pieces, P_SIZE // pieces, DH)


def attn(lens, q, g, kv, kr, vr):
    slots, heads = q.shape[0], q.shape[2] // DH
    n, _, piece, width = kv.shape
    rows = HEADS_STEP * ROWS
    column = lambda i, h, *_: (i, 0, h)
    slot = lambda i, h, *_: (i, 0, 0)
    return pl.pallas_call(
        functools.partial(attn_body, q.shape[2]),
        grid_spec=pltpu.PrefetchScalarGridSpec(
            num_scalar_prefetch=1,
            grid=(slots, heads // HEADS_STEP),
            in_specs=[
                pl.BlockSpec((1, L, HEADS_STEP * DH), column),
                pl.BlockSpec((1, L, HEADS_STEP * DH), column),
                pl.BlockSpec((n, 1, piece, DH), lambda i, h, *_: (0, i, 0, 0)),
                pl.BlockSpec((n, 1, piece, DH), lambda i, h, *_: (0, i, 0, 1)),
                pl.BlockSpec((1, L, DH), slot),
                pl.BlockSpec((1, L, DH), slot),
            ],
            out_specs=[
                pl.BlockSpec((1, L, HEADS_STEP * DH), column),
                pl.BlockSpec((1, L, DH), slot),
                pl.BlockSpec((1, L, DH), slot),
                pl.BlockSpec((n, 1, piece, width), lambda i, h, *_: (0, i, 0, 0)),
            ],
            scratch_shapes=[
                pltpu.VMEM((KEYS, 2 * DH), BF16),
                pltpu.VMEM((KEYS, DH), BF16),
                pltpu.VMEM((DH, KEYS), F32),
                pltpu.VMEM((DH, KEYS), F32),
            ]
            + [pltpu.VMEM((rows, KEYS), t) for t in (F32, F32, BF16, BF16)] * 2,
        ),
        out_shape=[
            jax.ShapeDtypeStruct(q.shape, BF16),
            jax.ShapeDtypeStruct(kr.shape, BF16),
            jax.ShapeDtypeStruct(vr.shape, BF16),
            jax.ShapeDtypeStruct(kv.shape, BF16),
        ],
        compiler_params=pltpu.CompilerParams(
            dimension_semantics=("arbitrary", "arbitrary"), vmem_limit_bytes=VMEM_ATTN
        ),
        name="attn_grads",
    )(lens, q, g, kv, kv, kr, vr)


def pick_body(owner, pieces_ref, out_ref):
    n, slots, piece, _ = out_ref.shape
    for d in range(n):
        for i in range(slots):
            out_ref[d, i] = pieces_ref[owner[d * slots + i], :piece]


def pick(owner, pieces, slots):
    n, rows, width = pieces.shape
    return pl.pallas_call(
        pick_body,
        grid_spec=pltpu.PrefetchScalarGridSpec(
            num_scalar_prefetch=1,
            grid=(1,),
            in_specs=[pl.BlockSpec((n, rows, width), lambda i, *_: (0, 0, 0))],
            out_specs=pl.BlockSpec((n, slots, rows - TAG, width), lambda i, *_: (0, 0, 0, 0)),
        ),
        out_shape=jax.ShapeDtypeStruct((n, slots, rows - TAG, width), BF16),
        compiler_params=pltpu.CompilerParams(vmem_limit_bytes=16 << 20),
        name="pick_pieces",
    )(owner, pieces)


def total_body(owner, part_ref, out_ref, acc):
    n, slots, _, _ = part_ref.shape
    acc[...] = jnp.zeros_like(acc)
    for d in range(n):
        for i in range(slots):
            acc[owner[d * slots + i]] += part_ref[d, i].astype(F32)
    out_ref[...] = acc[...].astype(BF16)


def totals(owner, partials):
    n, slots, piece, width = partials.shape
    return pl.pallas_call(
        total_body,
        grid_spec=pltpu.PrefetchScalarGridSpec(
            num_scalar_prefetch=1,
            grid=(1,),
            in_specs=[pl.BlockSpec((n, slots, piece, width), lambda i, *_: (0, 0, 0, 0))],
            out_specs=pl.BlockSpec((n, piece, width), lambda i, *_: (0, 0, 0)),
            scratch_shapes=[pltpu.VMEM((n, piece, width), F32)],
        ),
        out_shape=jax.ShapeDtypeStruct((n, piece, width), BF16),
        compiler_params=pltpu.CompilerParams(vmem_limit_bytes=16 << 20),
        name="sum_partials",
    )(owner, partials)


def per_device(resp_q, resp_k, resp_v, grad_out, prefix_keys, prefix_values, slot_prompt, resp_len):
    slots = resp_q.shape[0]
    n = lax.axis_size("prompt")
    piece = P_SIZE // n

    def exchange(x):
        return lax.all_to_all(x, "prompt", 0, 0, tiled=True)

    kv = jnp.concatenate([prefix_keys, prefix_values], 1).reshape(n, piece, 2 * DH)
    tag = jnp.zeros((n, TAG, 2 * DH), BF16) + jnp.pad(slot_prompt.astype(BF16), (0, 2 * DH - slots))
    pieces = exchange(jnp.concatenate([kv, tag], 1))
    owner = pieces[:, piece, :slots].astype(jnp.int32).reshape(n * slots)
    kv = exchange(pick(owner, pieces, slots))
    query_grad, resp_key_grad, resp_value_grad, partials = attn(resp_len, resp_q, grad_out, kv, resp_k, resp_v)
    sums = exchange(totals(owner, exchange(partials)))
    return (
        query_grad,
        resp_key_grad,
        resp_value_grad,
        sums[:, :, :DH].reshape(P_SIZE, DH),
        sums[:, :, DH:].reshape(P_SIZE, DH),
    )


def solution(mesh):
    placed = (
        P("prompt", None, "resp"),
        P("prompt", None, "resp"),
        P("prompt", None, "resp"),
        P("prompt", None, "resp"),
        P("prompt", "resp"),
        P("prompt", "resp"),
        P("prompt"),
        P("prompt"),
    )
    return jax.shard_map(
        per_device,
        mesh=mesh,
        in_specs=placed,
        out_specs=(
            P("prompt", None, "resp"),
            P("prompt", None, "resp"),
            P("prompt", None, "resp"),
            P("prompt", "resp"),
            P("prompt", "resp"),
        ),
        check_vma=False,
    )
```

```python
import functools
import math

import jax
import jax.numpy as jnp
from jax import lax
from jax.experimental import pallas as pl
from jax.experimental.pallas import tpu as pltpu
from jax.sharding import PartitionSpec as P

DH = 128
L = 512
P_SIZE = 1024
KEYS = P_SIZE + L
ROWS = 128
HEADS_STEP = 8
ROWS_SOFTMAX = 32
VMEM_ATTN = 46 << 20
TAG = 8
SCALE = 1.0 / math.sqrt(DH)
LOG2E = math.log2(math.e)
F32 = jnp.float32
BF16 = jnp.bfloat16


def dot(a, b, ca, cb):
    return lax.dot_general(a, b, (((ca,), (cb,)), ((), ())), preferred_element_type=F32)


def attn_body(width_q, q_ref, g_ref, kp_ref, vp_ref, kr_ref, vr_ref, dq_ref, dkr_ref, dvr_ref, part_ref, kf, vf, dk, dv, *buffers):
    group = pl.program_id(1)

    @pl.when(group == 0)
    def _():
        k_prefix = kp_ref[...].reshape(P_SIZE, DH)
        for side in range(2):
            kf[:P_SIZE, side * DH : (side + 1) * DH] = k_prefix
            kf[P_SIZE:, side * DH : (side + 1) * DH] = kr_ref[0]
        vf[:P_SIZE] = vp_ref[...].reshape(P_SIZE, DH)
        vf[P_SIZE:] = vr_ref[0]
        if HEADS_STEP * DH != width_q:
            dk[...] = jnp.zeros_like(dk)
            dv[...] = jnp.zeros_like(dv)

    rows = HEADS_STEP * ROWS
    masked = lax.broadcasted_iota(jnp.int32, (ROWS, ROWS), 1) > lax.broadcasted_iota(jnp.int32, (ROWS, ROWS), 0)
    for c in reversed(range(L // ROWS)):
        t0 = c * ROWS
        diag = P_SIZE + t0
        keys = diag + ROWS
        score, gprob, prob, dscore = [x.at[:, :keys] for x in buffers[4 * (c % 2) : 4 * (c % 2) + 4]]

        def stack(ref):
            return jnp.concatenate([ref[0, t0 : t0 + ROWS, h * DH : (h + 1) * DH] for h in range(HEADS_STEP)], 0)

        q = stack(q_ref)
        g = stack(g_ref)
        scaled = q.astype(F32) * (SCALE * LOG2E)
        high = scaled.astype(BF16)
        low = (scaled - high.astype(F32)).astype(BF16)
        score[...] = dot(jnp.concatenate([high, low], 1), kf[:keys], 1, 1)
        gprob[...] = dot(g, vf[:keys], 1, 1)
        for h in range(HEADS_STEP):
            span = slice(h * ROWS, (h + 1) * ROWS)
            score[span, diag:] = jnp.where(masked, -1e30, score[span, diag:])
        inverse = []
        for r in range(0, rows, ROWS_SOFTMAX):
            span = slice(r, r + ROWS_SOFTMAX)
            s = score[span]
            gp = gprob[span]
            e = jnp.exp2(s - jnp.max(s, axis=1, keepdims=True))
            inv = 1.0 / jnp.sum(e, axis=1, keepdims=True)
            row_dot = jnp.sum(e * gp, axis=1, keepdims=True) * inv
            prob[span] = e.astype(BF16)
            dscore[span] = (e * (gp - row_dot)).astype(BF16)
            inverse.append(jnp.broadcast_to(inv, (ROWS_SOFTMAX, DH)))
        inv = jnp.concatenate(inverse, 0)
        dv_part = dot((g.astype(F32) * inv).astype(BF16), prob[...], 0, 0)
        dk_part = dot((q.astype(F32) * inv).astype(BF16), dscore[...], 0, 0)
        if keys == KEYS and HEADS_STEP * DH == width_q:
            dv[...] = dv_part
            dk[...] = dk_part
        else:
            dv[:, :keys] += dv_part
            dk[:, :keys] += dk_part
        dq = (dot(dscore[...], kf[:keys, :DH], 1, 0) * (inv * SCALE)).astype(BF16)
        for h in range(HEADS_STEP):
            dq_ref[0, t0 : t0 + ROWS, h * DH : (h + 1) * DH] = dq[h * ROWS : (h + 1) * ROWS]

    @pl.when(group == pl.num_programs(1) - 1)
    def _():
        a = (dk[...] * SCALE).T.astype(BF16)
        b = dv[...].T.astype(BF16)
        dkr_ref[0] = a[P_SIZE:]
        dvr_ref[0] = b[P_SIZE:]
        pieces = part_ref.shape[0]
        part_ref[:, 0, :, :DH] = a[:P_SIZE].reshape(pieces, P_SIZE // pieces, DH)
        part_ref[:, 0, :, DH:] = b[:P_SIZE].reshape(pieces, P_SIZE // pieces, DH)


def attn(q, g, kv, kr, vr):
    slots, heads = q.shape[0], q.shape[2] // DH
    n, _, piece, width = kv.shape
    rows = HEADS_STEP * ROWS
    column = lambda i, h, *_: (i, 0, h)
    slot = lambda i, h, *_: (i, 0, 0)
    return pl.pallas_call(
        functools.partial(attn_body, q.shape[2]),
        grid_spec=pltpu.PrefetchScalarGridSpec(
            num_scalar_prefetch=0,
            grid=(slots, heads // HEADS_STEP),
            in_specs=[
                pl.BlockSpec((1, L, HEADS_STEP * DH), column),
                pl.BlockSpec((1, L, HEADS_STEP * DH), column),
                pl.BlockSpec((n, 1, piece, DH), lambda i, h, *_: (0, i, 0, 0)),
                pl.BlockSpec((n, 1, piece, DH), lambda i, h, *_: (0, i, 0, 1)),
                pl.BlockSpec((1, L, DH), slot),
                pl.BlockSpec((1, L, DH), slot),
            ],
            out_specs=[
                pl.BlockSpec((1, L, HEADS_STEP * DH), column),
                pl.BlockSpec((1, L, DH), slot),
                pl.BlockSpec((1, L, DH), slot),
                pl.BlockSpec((n, 1, piece, width), lambda i, h, *_: (0, i, 0, 0)),
            ],
            scratch_shapes=[
                pltpu.VMEM((KEYS, 2 * DH), BF16),
                pltpu.VMEM((KEYS, DH), BF16),
                pltpu.VMEM((DH, KEYS), F32),
                pltpu.VMEM((DH, KEYS), F32),
            ]
            + [pltpu.VMEM((rows, KEYS), t) for t in (F32, F32, BF16, BF16)] * 2,
        ),
        out_shape=[
            jax.ShapeDtypeStruct(q.shape, BF16),
            jax.ShapeDtypeStruct(kr.shape, BF16),
            jax.ShapeDtypeStruct(vr.shape, BF16),
            jax.ShapeDtypeStruct(kv.shape, BF16),
        ],
        compiler_params=pltpu.CompilerParams(
            dimension_semantics=("arbitrary", "arbitrary"), vmem_limit_bytes=VMEM_ATTN
        ),
        name="attn_grads",
    )(q, g, kv, kv, kr, vr)


def pick_body(owner, pieces_ref, out_ref):
    n, slots, piece, _ = out_ref.shape
    for d in range(n):
        for i in range(slots):
            out_ref[d, i] = pieces_ref[owner[d * slots + i], :piece]


def pick(owner, pieces, slots):
    n, rows, width = pieces.shape
    return pl.pallas_call(
        pick_body,
        grid_spec=pltpu.PrefetchScalarGridSpec(
            num_scalar_prefetch=1,
            grid=(1,),
            in_specs=[pl.BlockSpec((n, rows, width), lambda i, *_: (0, 0, 0))],
            out_specs=pl.BlockSpec((n, slots, rows - TAG, width), lambda i, *_: (0, 0, 0, 0)),
        ),
        out_shape=jax.ShapeDtypeStruct((n, slots, rows - TAG, width), BF16),
        compiler_params=pltpu.CompilerParams(vmem_limit_bytes=16 << 20),
        name="pick_pieces",
    )(owner, pieces)


def total_body(owner, part_ref, out_ref, acc):
    n, slots, _, _ = part_ref.shape
    acc[...] = jnp.zeros_like(acc)
    for d in range(n):
        for i in range(slots):
            acc[owner[d * slots + i]] += part_ref[d, i].astype(F32)
    out_ref[...] = acc[...].astype(BF16)


def totals(owner, partials):
    n, slots, piece, width = partials.shape
    return pl.pallas_call(
        total_body,
        grid_spec=pltpu.PrefetchScalarGridSpec(
            num_scalar_prefetch=1,
            grid=(1,),
            in_specs=[pl.BlockSpec((n, slots, piece, width), lambda i, *_: (0, 0, 0, 0))],
            out_specs=pl.BlockSpec((n, piece, width), lambda i, *_: (0, 0, 0)),
            scratch_shapes=[pltpu.VMEM((n, piece, width), F32)],
        ),
        out_shape=jax.ShapeDtypeStruct((n, piece, width), BF16),
        compiler_params=pltpu.CompilerParams(vmem_limit_bytes=16 << 20),
        name="sum_partials",
    )(owner, partials)


def per_device(resp_q, resp_k, resp_v, grad_out, prefix_keys, prefix_values, slot_prompt, resp_len):
    slots = resp_q.shape[0]
    n = lax.axis_size("prompt")
    piece = P_SIZE // n

    def exchange(x):
        return lax.all_to_all(x, "prompt", 0, 0, tiled=True)

    kv = jnp.concatenate([prefix_keys, prefix_values], 1).reshape(n, piece, 2 * DH)
    tag = jnp.zeros((n, TAG, 2 * DH), BF16) + jnp.pad(slot_prompt.astype(BF16), (0, 2 * DH - slots))
    pieces = exchange(jnp.concatenate([kv, tag], 1))
    valid = lax.broadcasted_iota(jnp.int32, (slots, L, 1), 1) < resp_len[:, None, None]
    masked = jnp.where(valid, grad_out, jnp.zeros_like(grad_out))
    owner = pieces[:, piece, :slots].astype(jnp.int32).reshape(n * slots)
    kv = exchange(pick(owner, pieces, slots))
    query_grad, resp_key_grad, resp_value_grad, partials = attn(resp_q, masked, kv, resp_k, resp_v)
    sums = exchange(totals(owner, exchange(partials)))
    return (
        query_grad,
        resp_key_grad,
        resp_value_grad,
        sums[:, :, :DH].reshape(P_SIZE, DH),
        sums[:, :, DH:].reshape(P_SIZE, DH),
    )


def solution(mesh):
    placed = (
        P("prompt", None, "resp"),
        P("prompt", None, "resp"),
        P("prompt", None, "resp"),
        P("prompt", None, "resp"),
        P("prompt", "resp"),
        P("prompt", "resp"),
        P("prompt"),
        P("prompt"),
    )
    return jax.shard_map(
        per_device,
        mesh=mesh,
        in_specs=placed,
        out_specs=(
            P("prompt", None, "resp"),
            P("prompt", None, "resp"),
            P("prompt", None, "resp"),
            P("prompt", "resp"),
            P("prompt", "resp"),
        ),
        check_vma=False,
    )
```
